32 devices in a mesh: dp: 8 (over z, x), mp: 4 (over y, core).
Axes of the slice: x: 2, y: 2, z: 4, core: 2. Of those that a mesh axis runs over, the one named last changes fastest.
Arguments:
- token_ids: int32 [512, 7], replicated, may hold values from 0 to 65535
- lengths: int32 [512], replicated, may hold values from 1 to 7, as said below
- pack_dest: int32 [512], replicated, may hold values from 0 to 7, as said below
- ref_hidden: bfloat16 [512, 7, 4096], P('dp', None, 'mp'), may hold values from -45 to 45
- reward_hidden: bfloat16 [512, 7, 4096], P('dp', None, 'mp'), may hold values from -140 to 140
- head_weight: bfloat16 [4096, 65536], P('mp', 'dp'), may hold values from -0.25 to 0.25
- norm_gain: float32 [4096], P('mp'), may hold values from 0.1 to 1.9
- score_weight: float32 [4096], P('mp'), may hold values from -0.09375 to 0.09375
- value_weight: float32 [4096], P('mp'), may hold values from -0.09375 to 0.09375
- old_logprob: float32 [2048], P('dp'), may hold values from -14 to -1
Outputs:
- ref_logprob: float32 [2048], P('dp')
- advantage: float32 [2048], P('dp')
The draws below stay inside these ranges and needn't reach their ends.
Inputs may be any that keep to these rules, and one draw needn't show every extreme that they name: `pack_dest`: request i belongs to request shard i // 64. Each request shard sends exactly 8 of its requests to every packed shard. A packed shard lists its requests by request shard, then by request index, and packs their tokens in that order from slot 0. In that order the requests of a packed shard form pairs whose lengths sum to 8, so every packed shard holds exactly 256 tokens; every packed shard has a request of length 1 and one of length 7.
All inputs are finite; a program needn't handle non-finite values.
Results may differ from the reference program's by a relative error of at most 0.0003.
Values may be sent and summed in bfloat16 or wider, within the bound.
A program may use at most 192 MiB of HBM per device.

```python
import math
import jax
import jax.numpy as jnp
import numpy as np
from jax import lax

D = 4096
VOCAB = 65536
MAXLEN = 7
REQ_DEV = 64
PROMPTS = 512
SLOT_DEV = 256
TOKENS = 2048


def routing_tables(key):
    shards = PROMPTS // REQ_DEV
    per_pair = REQ_DEV // shards
    source_keys = jax.random.split(jax.random.fold_in(key, 101), shards)
    orders = jax.vmap(lambda sub_key: jax.random.permutation(sub_key, REQ_DEV))(source_keys)
    target_shard = (jnp.arange(shards, dtype=jnp.int32)[:, None] + orders.astype(jnp.int32)) % shards
    same_shard = target_shard[:, :, None] == target_shard[:, None, :]
    earlier = jnp.arange(REQ_DEV)[None, :] < jnp.arange(REQ_DEV)[:, None]
    rank_in = jnp.sum(jnp.logical_and(same_shard, earlier[None]).astype(jnp.int32), axis=2).astype(jnp.int32)
    packed_pos = jnp.arange(shards, dtype=jnp.int32)[:, None] * per_pair + rank_in
    pair_count = REQ_DEV // 2
    first_len = jax.random.randint(jax.random.fold_in(key, 102), (shards, pair_count), 1, MAXLEN + 1)
    chosen = jax.random.randint(jax.random.fold_in(key, 103), (shards,), 0, pair_count)
    first_len = jnp.where(jnp.arange(pair_count)[None, :] == chosen[:, None], 1, first_len)
    packed = jnp.stack([first_len, MAXLEN + 1 - first_len], axis=2).reshape(shards * REQ_DEV).astype(jnp.int32)
    length = packed[(target_shard * REQ_DEV + packed_pos).reshape(-1)]
    return (target_shard.reshape(-1).astype(jnp.int32), length.astype(jnp.int32))


def draw_pack_dest(key, part):
    return routing_tables(key)[0]


def draw_lengths(key, part):
    return routing_tables(key)[1]


def draw_ref_hidden(key, part):
    full_shape = (PROMPTS, MAXLEN, D)
    values = jnp.clip(jax.random.normal(key, full_shape, jnp.float32), -6.0, 6.0)
    return values.astype(jnp.bfloat16)


def draw_reward_hidden(key, part):
    full_shape = (PROMPTS, MAXLEN, D)
    column = jnp.exp(math.log(10.0) * jnp.arange(D, dtype=jnp.float32) / D)
    values = jnp.clip(jax.random.normal(key, full_shape, jnp.float32), -6.0, 6.0) * column
    return values.astype(jnp.bfloat16)


def place_ends(entries, own_key, least, top_value):
    index_at = [jax.random.randint(jax.random.fold_in(own_key, axis), (), 0, length) for axis, length in enumerate(entries.shape)]
    main_axis = entries.shape.index(max(entries.shape))
    next_to = index_at[:main_axis] + [(index_at[main_axis] + 1) % entries.shape[main_axis]] + index_at[main_axis + 1:]
    return entries.at[tuple(index_at)].set(least).at[tuple(next_to)].set(top_value)


def level_of(stream_key, extent, cuts, low, high):
    loudness = 1.0
    for dim, blocks in cuts:
        heights = jax.random.uniform(jax.random.fold_in(jax.random.fold_in(stream_key, 6), dim), (blocks,), jnp.float32, low / len(cuts), high / len(cuts))
        loudness = loudness * jnp.repeat(jnp.exp(heights), extent[dim] // blocks).reshape((-1,) + (1,) * (len(extent) - 1 - dim))
    return loudness


def cumulative_ranks(count, slope):
    portions = [(1 << 20) // math.isqrt(standing ** slope) + 1 for standing in range(1, count + 1)]
    width = 1 + sum(portions) // (1 << 30)
    return np.cumsum(np.array([max(1, weight // width) for weight in portions]))


def skewed_ids(stream_key, extent, count, lean):
    listing = cumulative_ranks(count, lean)
    ticket = jax.random.randint(jax.random.fold_in(stream_key, 1), extent, 0, int(listing[count - 1]))
    standing = jnp.searchsorted(jnp.asarray(listing, jnp.int32), ticket, side="right")
    return jax.random.permutation(jax.random.fold_in(stream_key, 2), count)[standing].astype(jnp.int32)


def bell_draw(stream_key, shape, deviation, reach, cuts=(), kind=jnp.bfloat16):
    level = level_of(stream_key, shape, cuts, -0.22, 0.18) if cuts else 1.0
    array = jax.random.normal(stream_key, shape, jnp.float32) * deviation * level
    return jnp.minimum(jnp.maximum(array, -reach), reach).astype(kind)


def setup_inputs(seed: int = 0) -> dict:
    keys = jax.random.split(jax.random.key(seed), 11)
    return {
        "token_ids": place_ends(skewed_ids(keys[0], (PROMPTS, MAXLEN), VOCAB, 2), jax.random.fold_in(keys[0], 3), 0, VOCAB - 1).astype(jnp.int32),
        "lengths": draw_lengths(jax.random.fold_in(keys[10], 71), 0),
        "pack_dest": draw_pack_dest(jax.random.fold_in(keys[10], 71), 0),
        "ref_hidden": draw_ref_hidden(jax.random.fold_in(keys[10], 71), 0),
        "reward_hidden": draw_reward_hidden(jax.random.fold_in(keys[10], 71), 0),
        "head_weight": bell_draw(keys[5], (D, VOCAB), (D // 9) ** -0.5, 0.25, ((0, 4), (1, 8))),
        "norm_gain": jnp.clip(1.0 + 0.18 * jax.random.normal(keys[6], (D,), jnp.float32), 0.1, 1.9),
        "score_weight": bell_draw(keys[7], (D,), D ** -0.5, 0.09375, ((0, 4),), jnp.float32),
        "value_weight": bell_draw(keys[8], (D,), D ** -0.5, 0.09375, ((0, 4),), jnp.float32),
        "old_logprob": jnp.clip(-14.0 + 13.0 * jax.random.uniform(keys[9], (TOKENS,), jnp.float32) ** level_of(keys[9], (TOKENS,), ((0, 8),), -0.2, 0.2), -14.0, -1.0),
    }


kl_coef = 0.1
discount = 0.99
gae_mix = 0.95
norm_eps = 1e-05

def pack_tables(pack_dest, lengths, shards, req_dev, max_len, slot_dev):
    per_pair = req_dev // shards
    target_shard = pack_dest.reshape(shards, req_dev)
    same_shard = target_shard[:, :, None] == target_shard[:, None, :]
    earlier = jnp.arange(req_dev, dtype=jnp.int32)[None, :] < jnp.arange(req_dev, dtype=jnp.int32)[:, None]
    rank_in = lax.optimization_barrier(jnp.sum(jnp.logical_and(same_shard, earlier[None]).astype(jnp.int32), axis=2)).astype(jnp.int32)
    packed_pos = (jnp.arange(shards, dtype=jnp.int32)[:, None] * per_pair + rank_in).astype(jnp.int32)
    packed_place = (target_shard * req_dev + packed_pos).reshape(-1).astype(jnp.int32)
    source_of = jnp.zeros((shards * req_dev,), jnp.int32).at[packed_place].set(jnp.arange(shards * req_dev, dtype=jnp.int32)).reshape(shards, req_dev)
    packed_len = lengths[source_of].astype(jnp.int32)
    offsets = (jnp.cumsum(packed_len, axis=1, dtype=jnp.int32) - packed_len).astype(jnp.int32)
    slot_ids = jnp.arange(slot_dev, dtype=jnp.int32)
    request_at = (lax.optimization_barrier(jnp.sum((offsets[:, None, :] <= slot_ids[None, :, None]).astype(jnp.int32), axis=2)) - 1).astype(jnp.int32)
    start_at = jnp.take_along_axis(offsets, request_at, axis=1)
    offset_in = (slot_ids[None, :] - start_at).astype(jnp.int32)
    is_last = offset_in == jnp.take_along_axis(packed_len, request_at, axis=1) - 1
    source_prompt = jnp.take_along_axis(source_of, request_at, axis=1)
    return (target_shard, packed_pos, request_at, offset_in, is_last, source_prompt)

def advantages(reward, value_est, is_last, request_at):
    slot_count = reward.shape[0]
    next_value = jnp.concatenate([value_est[1:], jnp.zeros((1,), jnp.float32)])
    not_last = 1.0 - is_last.astype(jnp.float32)
    td_error = reward + discount * next_value * not_last - value_est
    slot_ids = jnp.arange(slot_count, dtype=jnp.int32)
    step_gap = (slot_ids[None, :] - slot_ids[:, None]).astype(jnp.float32)
    same_req = jnp.logical_and(request_at[:, None] == request_at[None, :], step_gap >= 0)
    weights = jnp.where(same_req, jnp.exp(jnp.maximum(step_gap, 0.0) * math.log(discount * gae_mix)), 0.0)
    return jnp.dot(weights, td_error, precision=lax.Precision.HIGHEST)

def reference(token_ids, lengths, pack_dest, ref_hidden, reward_hidden, head_weight, norm_gain, score_weight, value_weight, old_logprob):
    shards = PROMPTS // REQ_DEV
    target_shard, packed_pos, request_at, offset_in, is_last, source_prompt = pack_tables(pack_dest, lengths, shards, REQ_DEV, MAXLEN, SLOT_DEV)
    flat_rows = (source_prompt * MAXLEN + offset_in).reshape(-1).astype(jnp.int32)
    ref_rows = ref_hidden.reshape(PROMPTS * MAXLEN, D)[flat_rows]
    reward_rows = reward_hidden.reshape(PROMPTS * MAXLEN, D)[flat_rows]
    targets = token_ids.reshape(-1)[flat_rows]
    block_rows = math.gcd(TOKENS, 256)

    def score_block(inputs):
        row_block, id_block = inputs
        logits = jnp.dot(row_block, head_weight, preferred_element_type=jnp.float32)
        row_max = lax.optimization_barrier(jnp.max(logits, axis=1))
        exp_total = lax.optimization_barrier(jnp.sum(jnp.exp(logits - row_max[:, None]), axis=1))
        target_logit = jnp.take_along_axis(logits, id_block[:, None], axis=1)[:, 0]
        return target_logit - row_max - jnp.log(exp_total)
    ref_logprob = lax.map(score_block, (ref_rows.reshape(-1, block_rows, D), targets.reshape(-1, block_rows))).reshape(-1)
    hidden_f = reward_rows.astype(jnp.float32)
    squares = lax.optimization_barrier(jnp.sum(hidden_f * hidden_f, axis=1))
    score_dot = lax.optimization_barrier(jnp.sum(hidden_f * (norm_gain * score_weight), axis=1))
    value_dot = lax.optimization_barrier(jnp.sum(hidden_f * (norm_gain * value_weight), axis=1))
    inv_rms = lax.rsqrt(squares / D + norm_eps)
    score = (score_dot * inv_rms).reshape(shards, SLOT_DEV)
    value_est = (value_dot * inv_rms).reshape(shards, SLOT_DEV)
    reward = -kl_coef * (old_logprob.reshape(shards, SLOT_DEV) - ref_logprob.reshape(shards, SLOT_DEV)) + jnp.where(is_last, score, 0.0)
    advantage = jax.vmap(advantages)(reward, value_est, is_last, request_at)
    return (ref_logprob, advantage.reshape(-1))
```

```python
import functools

import jax
import jax.numpy as jnp
from jax import lax
from jax.experimental import pallas as pl
from jax.experimental.pallas import tpu as pltpu
from jax.sharding import PartitionSpec as P

kl_coef = 0.1
discount = 0.99
gae_mix = 0.95
norm_eps = 1e-05


def xor_order(a, axis, me):
    size = a.shape[axis]
    bit = 1
    while bit < size:
        shape = a.shape
        split = shape[:axis] + (size // (2 * bit), 2, bit) + shape[axis + 1 :]
        b = a.reshape(split)
        a = jnp.where((me & bit) != 0, jnp.flip(b, axis + 1), b).reshape(shape)
        bit *= 2
    return a


def send_xor(a, axis, k):
    size = lax.axis_size(axis)
    return lax.ppermute(a, axis, [(i, i ^ k) for i in range(size)])


def x_size(shards):
    x = 1
    while 2 * x * 2 * x <= shards:
        x *= 2
    return x


def score_kernel(terms, part_ref, target_ref, *refs):
    rows = refs[:terms]
    weights = refs[terms : 2 * terms]
    out_ref = refs[2 * terms]
    logits = part_ref[...]
    for a, w in zip(rows, weights):
        logits += jnp.dot(a[0], w[...], preferred_element_type=jnp.float32)
    count, vocab = logits.shape
    row_max = jnp.max(logits, axis=1, keepdims=True)
    exp_total = jnp.sum(jnp.exp(logits - row_max), axis=1, keepdims=True)
    column = lax.broadcasted_iota(jnp.int32, (count, vocab), 1)
    target = jnp.sum(jnp.where(column == target_ref[...], logits, 0.0), axis=1, keepdims=True)
    lane = lax.broadcasted_iota(jnp.int32, (count, 128), 1)
    packed = jnp.where(lane == 0, row_max, jnp.where(lane == 1, exp_total, target))
    out_ref[...] = packed.T[:8]


def score_rows(part, target, rows, weights):
    tokens, vocab = part.shape
    block = 256
    width = weights[0].shape[0]
    terms = len(rows)
    in_specs = [
        pl.BlockSpec((block, vocab), lambda i: (i, 0)),
        pl.BlockSpec((block, 1), lambda i: (i, 0)),
    ]
    for _, m in rows:
        in_specs.append(
            pl.BlockSpec((1, block, width), functools.partial(lambda m, i: (m, i, 0), m))
        )
    in_specs += [pl.BlockSpec((width, vocab), lambda i: (0, 0))] * terms
    return pl.pallas_call(
        functools.partial(score_kernel, terms),
        grid=(tokens // block,),
        in_specs=in_specs,
        out_specs=pl.BlockSpec((8, block), lambda i: (0, i)),
        out_shape=jax.ShapeDtypeStruct((8, tokens), jnp.float32),
        compiler_params=pltpu.CompilerParams(vmem_limit_bytes=50 * 1024 * 1024),
        cost_estimate=pl.CostEstimate(
            flops=2 * tokens * vocab * width * terms,
            bytes_accessed=tokens * vocab * 4 + terms * width * (tokens + vocab) * 2,
            transcendentals=tokens * vocab,
        ),
    )(part, target, *[a for a, _ in rows], *weights)


def combine_stats(stats):
    top = jnp.max(stats[:, 0], axis=0)
    total = jnp.sum(stats[:, 1] * jnp.exp(stats[:, 0] - top[None]), axis=0)
    return jnp.stack([top, total, jnp.sum(stats[:, 2], axis=0)])


def body(
    token_ids,
    lengths,
    pack_dest,
    ref_hidden,
    reward_hidden,
    head_weight,
    norm_gain,
    score_weight,
    value_weight,
    old_logprob,
):
    shards = lax.axis_size("dp")
    ways = lax.axis_size("mp")
    me = lax.axis_index("dp")
    part_index = lax.axis_index("mp")
    req_dev, max_len, width = ref_hidden.shape
    slots = req_dev // 2 * (max_len + 1)
    per_pair = req_dev // shards
    run = slots // shards
    tokens = shards * slots
    x_ways = x_size(shards)
    z_ways = shards // x_ways
    vocab_row = head_weight.shape[1]
    vocab = vocab_row // ways

    weight_parts = []
    for k in range(ways):
        own = lax.dynamic_slice(
            head_weight, (0, (part_index ^ k) * vocab), (width, vocab)
        )
        weight_parts.append(own if k == 0 else send_xor(own, "mp", k))

    dest = xor_order(pack_dest.reshape(shards, req_dev), 0, me)
    lens = xor_order(lengths.reshape(shards, req_dev), 0, me)
    ids = xor_order(token_ids.reshape(shards, req_dev * max_len), 0, me)
    index = jnp.arange(req_dev, dtype=jnp.int32)
    order = dest * req_dev + index[None]
    before = order[:, None, :] < order[:, :, None]
    offsets = jnp.sum(jnp.where(before, lens[:, None, :], 0), axis=2)
    inner = jnp.arange(max_len, dtype=jnp.int32)
    valid = inner < lens[:, :, None]
    place = jnp.where(valid, offsets[:, :, None] + inner, -1).reshape(shards, -1)
    last = (inner == lens[:, :, None] - 1).reshape(shards, -1)
    slot_ids = jnp.arange(slots, dtype=jnp.int32)
    chosen = place[:, None, :] == slot_ids[None, :, None]
    target_last = jnp.sum(
        jnp.where(chosen, (2 * ids + last.astype(jnp.int32))[:, None, :], 0), axis=2
    )
    targets = target_last >> 1
    is_last = target_last & 1

    own_chosen = chosen[0]
    rows = jnp.dot(
        own_chosen.astype(jnp.bfloat16),
        ref_hidden.reshape(req_dev * max_len, width),
        preferred_element_type=jnp.float32,
    ).astype(jnp.bfloat16)
    held = jnp.stack([rows] + [send_xor(rows, "mp", 2 * m) for m in range(1, ways // 2)])
    pieces = []
    for z in range(z_ways):
        got = held if z == 0 else send_xor(held, "dp", z * x_ways)
        for x in range(x_ways):
            pieces.append(got if x == 0 else send_xor(got, "dp", x))
    even = jnp.stack(pieces, axis=1).reshape(ways // 2, tokens, width)
    odd = send_xor(even, "mp", 1)

    hidden = reward_hidden.reshape(req_dev * max_len, width).astype(jnp.float32)
    sums = jnp.stack(
        [
            jnp.sum(hidden * hidden, axis=1),
            jnp.sum(hidden * (norm_gain * score_weight), axis=1),
            jnp.sum(hidden * (norm_gain * value_weight), axis=1),
        ]
    )
    sums = jnp.sum(jnp.where(own_chosen[None], sums[:, None, :], 0.0), axis=2)
    sums = lax.psum(sums, "mp")
    sums = lax.all_to_all(
        jnp.transpose(sums.reshape(3, shards, run), (1, 0, 2)), "dp", 0, 0, tiled=True
    )
    sums = jnp.transpose(sums, (1, 0, 2)).reshape(3, slots)
    inv_rms = lax.rsqrt(sums[0] / (width * ways) + norm_eps)
    score = sums[1] * inv_rms
    value_est = sums[2] * inv_rms
    my_last = lax.dynamic_slice(
        xor_order(is_last, 0, me), (0, me * run), (shards, run)
    ).reshape(slots)
    not_last = 1.0 - my_last.astype(jnp.float32)
    next_value = jnp.concatenate([value_est[1:], jnp.zeros((1,), jnp.float32)])
    fixed = (
        jnp.where(my_last != 0, score, 0.0)
        + discount * next_value * not_last
        - value_est
        - kl_coef * old_logprob
    )

    part = jnp.dot(even[0], weight_parts[0], preferred_element_type=jnp.float32)
    part += jnp.dot(odd[0], weight_parts[1], preferred_element_type=jnp.float32)
    base = me * vocab_row + part_index * vocab
    stats = score_rows(
        part,
        (targets - base).reshape(tokens, 1),
        [(a, m) for m in range(1, ways // 2) for a in (even, odd)],
        weight_parts[2:],
    )[:3]

    stats = xor_order(stats.reshape(3, shards, shards, run), 1, me)
    stats = lax.all_to_all(jnp.transpose(stats, (2, 0, 1, 3)), "dp", 0, 0, tiled=True)
    stats = combine_stats(stats.reshape(shards, 3, slots))
    stats = combine_stats(lax.all_gather(stats, "mp"))
    ref_logprob = stats[2] - stats[0] - jnp.log(stats[1])

    td_error = fixed + kl_coef * ref_logprob
    decay = discount * gae_mix * not_last
    advantage = td_error
    for _ in range(max_len - 1):
        following = jnp.concatenate([advantage[1:], jnp.zeros((1,), jnp.float32)])
        advantage = td_error + decay * following
    return (ref_logprob, advantage)


def solution(mesh):
    return jax.shard_map(
        body,
        mesh=mesh,
        in_specs=(
            P(),
            P(),
            P(),
            P("dp", None, "mp"),
            P("dp", None, "mp"),
            P("mp", "dp"),
            P("mp"),
            P("mp"),
            P("mp"),
            P("dp"),
        ),
        out_specs=(P("dp"), P("dp")),
        check_vma=False,
    )
```

```python
import functools

import jax
import jax.numpy as jnp
from jax import lax
from jax.experimental import pallas as pl
from jax.experimental.pallas import tpu as pltpu
from jax.sharding import PartitionSpec as P

kl_coef = 0.1
discount = 0.99
gae_mix = 0.95
norm_eps = 1e-05


def xor_order(a, axis, me):
    size = a.shape[axis]
    bit = 1
    while bit < size:
        shape = a.shape
        split = shape[:axis] + (size // (2 * bit), 2, bit) + shape[axis + 1 :]
        b = a.reshape(split)
        a = jnp.where((me & bit) != 0, jnp.flip(b, axis + 1), b).reshape(shape)
        bit *= 2
    return a


def flip(a, k):
    bit = 1
    while bit <= k:
        if k & bit:
            a = a + bit - 2 * bit * ((a // bit) % 2)
        bit *= 2
    return a


def x_size(shards):
    x = 1
    while 2 * x * 2 * x <= shards:
        x *= 2
    return x


def exchange_kernel(
    shards, ways, rows_ref, weight_ref, held, got, part, w_scratch,
    y_sems, z_sems, x_sems, c_sems, w_sems, local_sems,
):
    me = lax.axis_index("dp")
    place = lax.axis_index("mp")
    x_ways = x_size(shards)
    z_ways = shards // x_ways
    halves = ways // 2
    slots, width = rows_ref.shape
    tokens = held.shape[1]
    vocab = got.shape[2]

    peers = [{"mp": flip(place, k)} for k in range(1, ways)]
    peers += [{"dp": flip(me, z * x_ways)} for z in range(1, z_ways)]
    peers += [{"dp": flip(me, x)} for x in range(1, x_ways)]
    barrier = pltpu.get_barrier_semaphore()
    for peer in peers:
        pl.semaphore_signal(
            barrier, inc=1, device_id=peer, device_id_type=pl.DeviceIdType.MESH
        )
    pl.semaphore_wait(barrier, len(peers))

    started = []

    def send(src, dst, sems, i, peer):
        copy = pltpu.make_async_remote_copy(
            src_ref=src,
            dst_ref=dst,
            send_sem=sems.at[0, i],
            recv_sem=sems.at[1, i],
            device_id=peer,
            device_id_type=pl.DeviceIdType.MESH,
        )
        copy.start()
        started.append(copy)
        return copy

    def slot(k, r, count=1):
        return held.at[k, pl.ds(r * slots, count * slots), :]

    def columns(k):
        return weight_ref.at[:, pl.ds(pl.multiple_of(flip(place, k) * vocab, vocab), vocab)]

    own_rows = pltpu.make_async_copy(rows_ref, slot(0, 0), local_sems.at[0])
    own_rows.start()
    y_copy, z_copy, x_copy, c_copy, w_copy = {}, {}, {}, {}, {}
    for m in range(1, halves):
        y_copy[m] = send(rows_ref, slot(2 * m, 0), y_sems, m, {"mp": flip(place, 2 * m)})
    for k in list(range(2, ways)) + [1]:
        w_copy[k] = send(columns(k), got.at[k - 1], w_sems, k, {"mp": flip(place, k)})
    own_weight = pltpu.make_async_copy(columns(0), w_scratch.at[0], local_sems.at[1])
    own_weight.start()

    def spread(m, z):
        src = rows_ref if m == 0 and z == 0 else slot(2 * m, z * x_ways)
        if z == 0:
            for z_to in range(1, z_ways):
                z_copy[m, z_to] = send(
                    src, slot(2 * m, z_to * x_ways), z_sems, m * z_ways + z_to,
                    {"dp": flip(me, z_to * x_ways)},
                )
        for x in range(1, x_ways):
            x_copy[m, z, x] = send(
                src, slot(2 * m, z * x_ways + x), x_sems, (m * z_ways + z) * x_ways + x,
                {"dp": flip(me, x)},
            )

    spread(0, 0)
    for m in range(1, halves):
        y_copy[m].wait_recv()
        spread(m, 0)
    for z in range(1, z_ways):
        for m in range(halves):
            z_copy[m, z].wait_recv()
            spread(m, z)
    own_rows.wait()
    for z in range(z_ways):
        for m in range(halves):
            for x in range(1, x_ways):
                x_copy[m, z, x].wait_recv()
            c_copy[m, z] = send(
                slot(2 * m, z * x_ways, x_ways), slot(2 * m + 1, z * x_ways, x_ways),
                c_sems, m * z_ways + z, {"mp": flip(place, 1)},
            )
    own_weight.wait()
    w_copy[1].wait_recv()
    next_weight = pltpu.make_async_copy(got.at[0], w_scratch.at[1], local_sems.at[2])
    next_weight.start()
    next_weight.wait()
    for c in c_copy.values():
        c.wait_recv()

    def multiply(a_ref, b_ref, out_ref):
        out_ref[...] = jnp.dot(
            a_ref[...], w_scratch[0], preferred_element_type=jnp.float32
        ) + jnp.dot(b_ref[...], w_scratch[1], preferred_element_type=jnp.float32)

    block = 256
    pltpu.emit_pipeline(
        multiply,
        grid=(tokens // block,),
        in_specs=[pl.BlockSpec((block, width), lambda i: (i, 0))] * 2,
        out_specs=[pl.BlockSpec((block, vocab), lambda i: (i, 0))],
    )(held.at[0], held.at[1], part)
    for k in range(2, ways):
        w_copy[k].wait_recv()
    for copy in started:
        copy.wait_send()


def exchange(rows, head_weight, shards, ways):
    slots, width = rows.shape
    tokens = shards * slots
    vocab = head_weight.shape[1] // ways
    halves = ways // 2
    pairs = lambda count: pltpu.SemaphoreType.DMA((2, count))
    return pl.pallas_call(
        functools.partial(exchange_kernel, shards, ways),
        in_specs=[pl.BlockSpec(memory_space=pl.ANY)] * 2,
        out_specs=[pl.BlockSpec(memory_space=pl.ANY)] * 3,
        out_shape=[
            jax.ShapeDtypeStruct((ways, tokens, width), rows.dtype),
            jax.ShapeDtypeStruct((ways - 1, width, vocab), head_weight.dtype),
            jax.ShapeDtypeStruct((tokens, vocab), jnp.float32),
        ],
        scratch_shapes=[
            pltpu.VMEM((2, width, vocab), head_weight.dtype),
            pairs(halves),
            pairs(halves * shards),
            pairs(halves * shards),
            pairs(halves * shards),
            pairs(ways),
            pltpu.SemaphoreType.DMA((3,)),
        ],
        compiler_params=pltpu.CompilerParams(
            collective_id=0, has_side_effects=True, vmem_limit_bytes=48 * 1024 * 1024
        ),
        cost_estimate=pl.CostEstimate(
            flops=4 * tokens * vocab * width,
            bytes_accessed=2 * ways * width * (tokens + vocab) + 4 * tokens * vocab,
            transcendentals=0,
        ),
    )(rows, head_weight)


def score_kernel(terms, part_ref, target_ref, *refs):
    rows = refs[:terms]
    weights = refs[terms : 2 * terms]
    out_ref = refs[2 * terms]
    logits = part_ref[...]
    for a, w in zip(rows, weights):
        logits += jnp.dot(a[0], w[0], preferred_element_type=jnp.float32)
    count, vocab = logits.shape
    row_max = jnp.max(logits, axis=1, keepdims=True)
    exp_total = jnp.sum(jnp.exp(logits - row_max), axis=1, keepdims=True)
    column = lax.broadcasted_iota(jnp.int32, (count, vocab), 1)
    target = jnp.sum(jnp.where(column == target_ref[...], logits, 0.0), axis=1, keepdims=True)
    lane = lax.broadcasted_iota(jnp.int32, (count, 128), 1)
    packed = jnp.where(lane == 0, row_max, jnp.where(lane == 1, exp_total, target))
    out_ref[...] = packed.T[:8]


def score_rows(part, target, held, got):
    tokens, vocab = part.shape
    block = 256
    ways, _, width = held.shape
    terms = ways - 2
    in_specs = [
        pl.BlockSpec((block, vocab), lambda i: (i, 0)),
        pl.BlockSpec((block, 1), lambda i: (i, 0)),
    ]
    for k in range(2, ways):
        in_specs.append(
            pl.BlockSpec((1, block, width), functools.partial(lambda k, i: (k, i, 0), k))
        )
    for k in range(2, ways):
        in_specs.append(
            pl.BlockSpec((1, width, vocab), functools.partial(lambda k, i: (k - 1, 0, 0), k))
        )
    return pl.pallas_call(
        functools.partial(score_kernel, terms),
        grid=(tokens // block,),
        in_specs=in_specs,
        out_specs=pl.BlockSpec((8, block), lambda i: (0, i)),
        out_shape=jax.ShapeDtypeStruct((8, tokens), jnp.float32),
        compiler_params=pltpu.CompilerParams(vmem_limit_bytes=50 * 1024 * 1024),
        cost_estimate=pl.CostEstimate(
            flops=2 * tokens * vocab * width * terms,
            bytes_accessed=tokens * vocab * 4 + terms * width * (tokens + vocab) * 2,
            transcendentals=tokens * vocab,
        ),
    )(part, target, *[held] * terms, *[got] * terms)


def combine_stats(stats):
    top = jnp.max(stats[:, 0], axis=0)
    total = jnp.sum(stats[:, 1] * jnp.exp(stats[:, 0] - top[None]), axis=0)
    return jnp.stack([top, total, jnp.sum(stats[:, 2], axis=0)])


def body(
    token_ids,
    lengths,
    pack_dest,
    ref_hidden,
    reward_hidden,
    head_weight,
    norm_gain,
    score_weight,
    value_weight,
    old_logprob,
):
    shards = lax.axis_size("dp")
    ways = lax.axis_size("mp")
    me = lax.axis_index("dp")
    part_index = lax.axis_index("mp")
    req_dev, max_len, width = ref_hidden.shape
    slots = req_dev // 2 * (max_len + 1)
    per_pair = req_dev // shards
    run = slots // shards
    tokens = shards * slots
    vocab_row = head_weight.shape[1]
    vocab = vocab_row // ways

    dest = xor_order(pack_dest.reshape(shards, req_dev), 0, me)
    lens = xor_order(lengths.reshape(shards, req_dev), 0, me)
    ids = xor_order(token_ids.reshape(shards, req_dev * max_len), 0, me)
    index = jnp.arange(req_dev, dtype=jnp.int32)
    order = dest * req_dev + index[None]
    before = order[:, None, :] < order[:, :, None]
    offsets = jnp.sum(jnp.where(before, lens[:, None, :], 0), axis=2)
    inner = jnp.arange(max_len, dtype=jnp.int32)
    valid = inner < lens[:, :, None]
    place = jnp.where(valid, offsets[:, :, None] + inner, -1).reshape(shards, -1)
    last = (inner == lens[:, :, None] - 1).reshape(shards, -1)
    slot_ids = jnp.arange(slots, dtype=jnp.int32)
    chosen = place[:, None, :] == slot_ids[None, :, None]
    target_last = jnp.sum(
        jnp.where(chosen, (2 * ids + last.astype(jnp.int32))[:, None, :], 0), axis=2
    )
    targets = target_last >> 1
    is_last = target_last & 1

    own_chosen = chosen[0]
    rows = jnp.dot(
        own_chosen.astype(jnp.bfloat16),
        ref_hidden.reshape(req_dev * max_len, width),
        preferred_element_type=jnp.float32,
    ).astype(jnp.bfloat16)
    held, got, part = exchange(rows, head_weight, shards, ways)

    hidden = reward_hidden.reshape(req_dev * max_len, width).astype(jnp.float32)
    sums = jnp.stack(
        [
            jnp.sum(hidden * hidden, axis=1),
            jnp.sum(hidden * (norm_gain * score_weight), axis=1),
            jnp.sum(hidden * (norm_gain * value_weight), axis=1),
        ]
    )
    sums = jnp.sum(jnp.where(own_chosen[None], sums[:, None, :], 0.0), axis=2)
    my_last = lax.dynamic_slice(
        xor_order(is_last, 0, me), (0, me * run), (shards, run)
    ).reshape(slots)
    not_last = 1.0 - my_last.astype(jnp.float32)
    base = me * vocab_row + part_index * vocab
    stats = score_rows(part, (targets - base).reshape(tokens, 1), held, got)[:3]

    stats = xor_order(stats.reshape(3, shards, shards, run), 1, me)
    sent = jnp.concatenate([stats, sums.reshape(3, 1, shards, run)], axis=1)
    taken = lax.all_to_all(jnp.transpose(sent, (2, 0, 1, 3)), "dp", 0, 0, tiled=True)
    stats = combine_stats(taken[:, :, :shards].reshape(shards, 3, slots))
    sums = jnp.transpose(taken[:, :, shards], (1, 0, 2)).reshape(3, slots)
    gathered = lax.all_gather(jnp.concatenate([stats, sums]), "mp")
    stats = combine_stats(gathered[:, :3])
    sums = jnp.sum(gathered[:, 3:], axis=0)
    ref_logprob = stats[2] - stats[0] - jnp.log(stats[1])

    inv_rms = lax.rsqrt(sums[0] / (width * ways) + norm_eps)
    score = sums[1] * inv_rms
    value_est = sums[2] * inv_rms
    next_value = jnp.concatenate([value_est[1:], jnp.zeros((1,), jnp.float32)])
    reward = -kl_coef * (old_logprob - ref_logprob) + jnp.where(my_last != 0, score, 0.0)
    td_error = reward + discount * next_value * not_last - value_est
    decay = discount * gae_mix * not_last
    advantage = td_error
    for _ in range(max_len - 1):
        following = jnp.concatenate([advantage[1:], jnp.zeros((1,), jnp.float32)])
        advantage = td_error + decay * following
    return (ref_logprob, advantage)


def solution(mesh):
    return jax.shard_map(
        body,
        mesh=mesh,
        in_specs=(
            P(),
            P(),
            P(),
            P("dp", None, "mp"),
            P("dp", None, "mp"),
            P("mp", "dp"),
            P("mp"),
            P("mp"),
            P("mp"),
            P("dp"),
        ),
        out_specs=(P("dp"), P("dp")),
        check_vma=False,
    )
```

```python
import functools

import jax
import jax.numpy as jnp
from jax import lax
from jax.experimental import pallas as pl
from jax.experimental.pallas import tpu as pltpu
from jax.sharding import PartitionSpec as P

kl_coef = 0.1
discount = 0.99
gae_mix = 0.95
norm_eps = 1e-05


def xor_order(a, axis, me):
    size = a.shape[axis]
    bit = 1
    while bit < size:
        shape = a.shape
        split = shape[:axis] + (size // (2 * bit), 2, bit) + shape[axis + 1 :]
        b = a.reshape(split)
        a = jnp.where((me & bit) != 0, jnp.flip(b, axis + 1), b).reshape(shape)
        bit *= 2
    return a


def flip(a, k):
    bit = 1
    while bit <= k:
        if k & bit:
            a = a + bit - 2 * bit * ((a // bit) % 2)
        bit *= 2
    return a


def x_size(shards):
    x = 1
    while 2 * x * 2 * x <= shards:
        x *= 2
    return x


def score_block(logits, target, first, out_ref):
    count, vocab = logits.shape
    row_max = jnp.max(logits, axis=1, keepdims=True)
    exp_total = jnp.sum(jnp.exp(logits - row_max), axis=1, keepdims=True)
    column = lax.broadcasted_iota(jnp.int32, (count, vocab), 1) + first
    picked = jnp.sum(jnp.where(column == target, logits, 0.0), axis=1, keepdims=True)
    lane = lax.broadcasted_iota(jnp.int32, (count, 128), 1)
    packed = jnp.where(lane == 0, row_max, jnp.where(lane == 1, exp_total, picked))
    out_ref[0] = packed.T[:8]


def exchange_kernel(
    shards, ways, rows_ref, weight_ref, target_ref, held, near, far, part, stats,
    w_near, w_far,
    y_sems, z_sems, x_sems, c_sems, w_sems, f_sems, local_sems,
):
    me = lax.axis_index("dp")
    place = lax.axis_index("mp")
    x_ways = x_size(shards)
    z_ways = shards // x_ways
    halves = ways // 2
    slots, width = rows_ref.shape
    tokens = held.shape[1]
    vocab = near.shape[1]
    cuts, _, _, cut = far.shape

    peers = [{"mp": flip(place, k)} for k in range(1, ways)]
    peers += [{"dp": flip(me, z * x_ways)} for z in range(1, z_ways)]
    peers += [{"dp": flip(me, x)} for x in range(1, x_ways)]
    barrier = pltpu.get_barrier_semaphore()
    for peer in peers:
        pl.semaphore_signal(
            barrier, inc=1, device_id=peer, device_id_type=pl.DeviceIdType.MESH
        )
    pl.semaphore_wait(barrier, len(peers))

    started = []

    def send(src, dst, sems, i, peer):
        copy = pltpu.make_async_remote_copy(
            src_ref=src,
            dst_ref=dst,
            send_sem=sems.at[0, i],
            recv_sem=sems.at[1, i],
            device_id=peer,
            device_id_type=pl.DeviceIdType.MESH,
        )
        copy.start()
        started.append(copy)
        return copy

    def slot(k, r, count=1):
        return held.at[k, pl.ds(r * slots, count * slots), :]

    def columns(k, first=0, count=vocab):
        start = pl.multiple_of(flip(place, k) * vocab + first, count)
        return weight_ref.at[:, pl.ds(start, count)]

    def send_far(c):
        for k in range(2, ways):
            far_copy[c, k] = send(
                columns(k, c * cut, cut), far.at[c, k - 2], f_sems, c * ways + k,
                {"mp": flip(place, k)},
            )

    own_rows = pltpu.make_async_copy(rows_ref, slot(0, 0), local_sems.at[0])
    own_rows.start()
    y_copy, z_copy, x_copy, c_copy, far_copy = {}, {}, {}, {}, {}
    for m in range(1, halves):
        y_copy[m] = send(rows_ref, slot(2 * m, 0), y_sems, m, {"mp": flip(place, 2 * m)})
    for c in range(max(1, cuts - 1)):
        send_far(c)
    near_copy = send(columns(1), near, w_sems, 0, {"mp": flip(place, 1)})
    own_weight = pltpu.make_async_copy(columns(0), w_near.at[0], local_sems.at[1])
    own_weight.start()

    def spread(m, z):
        src = rows_ref if m == 0 and z == 0 else slot(2 * m, z * x_ways)
        if z == 0:
            for z_to in range(1, z_ways):
                z_copy[m, z_to] = send(
                    src, slot(2 * m, z_to * x_ways), z_sems, m * z_ways + z_to,
                    {"dp": flip(me, z_to * x_ways)},
                )
        for x in range(1, x_ways):
            x_copy[m, z, x] = send(
                src, slot(2 * m, z * x_ways + x), x_sems, (m * z_ways + z) * x_ways + x,
                {"dp": flip(me, x)},
            )

    spread(0, 0)
    for m in range(1, halves):
        y_copy[m].wait_recv()
        spread(m, 0)
    for z in range(1, z_ways):
        for m in range(halves):
            z_copy[m, z].wait_recv()
            spread(m, z)
    own_rows.wait()
    for z in range(z_ways):
        for m in range(halves):
            for x in range(1, x_ways):
                x_copy[m, z, x].wait_recv()
            c_copy[m, z] = send(
                slot(2 * m, z * x_ways, x_ways), slot(2 * m + 1, z * x_ways, x_ways),
                c_sems, m * z_ways + z, {"mp": flip(place, 1)},
            )
    if cuts > 1:
        send_far(cuts - 1)
    own_weight.wait()
    near_copy.wait_recv()
    near_weight = pltpu.make_async_copy(near, w_near.at[1], local_sems.at[2])
    near_weight.start()
    near_weight.wait()
    for c in c_copy.values():
        c.wait_recv()

    block = 256
    steps = (tokens // block,)
    row_spec = pl.BlockSpec((block, width), lambda i: (i, 0))

    def multiply(a_ref, b_ref, out_ref):
        out_ref[...] = jnp.dot(
            a_ref[...], w_near[0], preferred_element_type=jnp.float32
        ) + jnp.dot(b_ref[...], w_near[1], preferred_element_type=jnp.float32)

    pltpu.emit_pipeline(
        multiply,
        grid=steps,
        in_specs=[row_spec] * 2,
        out_specs=[pl.BlockSpec((block, vocab), lambda i: (i, 0))],
    )(held.at[0], held.at[1], part)

    for c in range(cuts):
        for k in range(2, ways):
            far_copy[c, k].wait_recv()
        load = pltpu.make_async_copy(far.at[c], w_far, local_sems.at[3])
        load.start()
        load.wait()

        def score(part_block, target_block, *refs, first=c * cut):
            logits = part_block[...]
            for k in range(ways - 2):
                logits += jnp.dot(refs[k][...], w_far[k], preferred_element_type=jnp.float32)
            score_block(logits, target_block[...], first, refs[-1])

        pltpu.emit_pipeline(
            score,
            grid=steps,
            in_specs=[
                pl.BlockSpec((block, cut), functools.partial(lambda c, i: (i, c), c)),
                pl.BlockSpec((block, 1), lambda i: (i, 0)),
            ]
            + [row_spec] * (ways - 2),
            out_specs=[pl.BlockSpec((1, 8, block), functools.partial(lambda c, i: (c, 0, i), c))],
        )(part, target_ref, *[held.at[k] for k in range(2, ways)], stats)
    for copy in started:
        copy.wait_send()


def score_rows(rows, head_weight, target, shards, ways):
    slots, width = rows.shape
    tokens = shards * slots
    vocab = head_weight.shape[1] // ways
    halves = ways // 2
    cut = min(vocab, 512)
    cuts = vocab // cut
    pairs = lambda count: pltpu.SemaphoreType.DMA((2, count))
    return pl.pallas_call(
        functools.partial(exchange_kernel, shards, ways),
        in_specs=[pl.BlockSpec(memory_space=pl.ANY)] * 3,
        out_specs=[pl.BlockSpec(memory_space=pl.ANY)] * 5,
        out_shape=[
            jax.ShapeDtypeStruct((ways, tokens, width), rows.dtype),
            jax.ShapeDtypeStruct((width, vocab), head_weight.dtype),
            jax.ShapeDtypeStruct((cuts, ways - 2, width, cut), head_weight.dtype),
            jax.ShapeDtypeStruct((tokens, vocab), jnp.float32),
            jax.ShapeDtypeStruct((cuts, 8, tokens), jnp.float32),
        ],
        scratch_shapes=[
            pltpu.VMEM((2, width, vocab), head_weight.dtype),
            pltpu.VMEM((ways - 2, width, cut), head_weight.dtype),
            pairs(halves),
            pairs(halves * shards),
            pairs(halves * shards),
            pairs(halves * shards),
            pairs(1),
            pairs(cuts * ways),
            pltpu.SemaphoreType.DMA((4,)),
        ],
        compiler_params=pltpu.CompilerParams(
            collective_id=0, has_side_effects=True, vmem_limit_bytes=48 * 1024 * 1024
        ),
        cost_estimate=pl.CostEstimate(
            flops=2 * ways * tokens * vocab * width,
            bytes_accessed=2 * ways * width * (tokens + vocab) + 8 * tokens * vocab,
            transcendentals=tokens * vocab,
        ),
    )(rows, head_weight, target)[4]


def combine_stats(stats):
    top = jnp.max(stats[:, 0], axis=0)
    total = jnp.sum(stats[:, 1] * jnp.exp(stats[:, 0] - top[None]), axis=0)
    return jnp.stack([top, total, jnp.sum(stats[:, 2], axis=0)])


def body(
    token_ids,
    lengths,
    pack_dest,
    ref_hidden,
    reward_hidden,
    head_weight,
    norm_gain,
    score_weight,
    value_weight,
    old_logprob,
):
    shards = lax.axis_size("dp")
    ways = lax.axis_size("mp")
    me = lax.axis_index("dp")
    part_index = lax.axis_index("mp")
    req_dev, max_len, width = ref_hidden.shape
    slots = req_dev // 2 * (max_len + 1)
    per_pair = req_dev // shards
    run = slots // shards
    tokens = shards * slots
    vocab_row = head_weight.shape[1]
    vocab = vocab_row // ways

    dest = xor_order(pack_dest.reshape(shards, req_dev), 0, me)
    lens = xor_order(lengths.reshape(shards, req_dev), 0, me)
    ids = xor_order(token_ids.reshape(shards, req_dev * max_len), 0, me)
    index = jnp.arange(req_dev, dtype=jnp.int32)
    order = dest * req_dev + index[None]
    before = order[:, None, :] < order[:, :, None]
    offsets = jnp.sum(jnp.where(before, lens[:, None, :], 0), axis=2)
    inner = jnp.arange(max_len, dtype=jnp.int32)
    valid = inner < lens[:, :, None]
    place = jnp.where(valid, offsets[:, :, None] + inner, -1).reshape(shards, -1)
    last = (inner == lens[:, :, None] - 1).reshape(shards, -1)
    slot_ids = jnp.arange(slots, dtype=jnp.int32)
    chosen = place[:, None, :] == slot_ids[None, :, None]
    target_last = jnp.sum(
        jnp.where(chosen, (2 * ids + last.astype(jnp.int32))[:, None, :], 0), axis=2
    )
    targets = target_last >> 1
    is_last = target_last & 1

    own_chosen = chosen[0]
    rows = jnp.dot(
        own_chosen.astype(jnp.bfloat16),
        ref_hidden.reshape(req_dev * max_len, width),
        preferred_element_type=jnp.float32,
    ).astype(jnp.bfloat16)
    hidden = reward_hidden.reshape(req_dev * max_len, width).astype(jnp.float32)
    sums = jnp.stack(
        [
            jnp.sum(hidden * hidden, axis=1),
            jnp.sum(hidden * (norm_gain * score_weight), axis=1),
            jnp.sum(hidden * (norm_gain * value_weight), axis=1),
        ]
    )
    sums = jnp.sum(jnp.where(own_chosen[None], sums[:, None, :], 0.0), axis=2)
    my_last = lax.dynamic_slice(
        xor_order(is_last, 0, me), (0, me * run), (shards, run)
    ).reshape(slots)
    not_last = 1.0 - my_last.astype(jnp.float32)
    base = me * vocab_row + part_index * vocab
    stats = score_rows(
        rows, head_weight, (targets - base).reshape(tokens, 1), shards, ways
    )
    stats = combine_stats(stats[:, :3])

    stats = xor_order(stats.reshape(3, shards, shards, run), 1, me)
    sent = jnp.concatenate([stats, sums.reshape(3, 1, shards, run)], axis=1)
    taken = lax.all_to_all(jnp.transpose(sent, (2, 0, 1, 3)), "dp", 0, 0, tiled=True)
    stats = combine_stats(taken[:, :, :shards].reshape(shards, 3, slots))
    sums = jnp.transpose(taken[:, :, shards], (1, 0, 2)).reshape(3, slots)
    gathered = lax.all_gather(jnp.concatenate([stats, sums]), "mp")
    stats = combine_stats(gathered[:, :3])
    sums = jnp.sum(gathered[:, 3:], axis=0)
    ref_logprob = stats[2] - stats[0] - jnp.log(stats[1])

    inv_rms = lax.rsqrt(sums[0] / (width * ways) + norm_eps)
    score = sums[1] * inv_rms
    value_est = sums[2] * inv_rms
    next_value = jnp.concatenate([value_est[1:], jnp.zeros((1,), jnp.float32)])
    reward = -kl_coef * (old_logprob - ref_logprob) + jnp.where(my_last != 0, score, 0.0)
    td_error = reward + discount * next_value * not_last - value_est
    decay = discount * gae_mix * not_last
    advantage = td_error
    for _ in range(max_len - 1):
        following = jnp.concatenate([advantage[1:], jnp.zeros((1,), jnp.float32)])
        advantage = td_error + decay * following
    return (ref_logprob, advantage)


def solution(mesh):
    return jax.shard_map(
        body,
        mesh=mesh,
        in_specs=(
            P(),
            P(),
            P(),
            P("dp", None, "mp"),
            P("dp", None, "mp"),
            P("mp", "dp"),
            P("mp"),
            P("mp"),
            P("mp"),
            P("dp"),
        ),
        out_specs=(P("dp"), P("dp")),
        check_vma=False,
    )
```

```python
import functools

import jax
import jax.numpy as jnp
from jax import lax
from jax.experimental import pallas as pl
from jax.experimental.pallas import tpu as pltpu
from jax.sharding import PartitionSpec as P

kl_coef = 0.1
discount = 0.99
gae_mix = 0.95
norm_eps = 1e-05


def xor_order(a, axis, me):
    size = a.shape[axis]
    bit = 1
    while bit < size:
        shape = a.shape
        split = shape[:axis] + (size // (2 * bit), 2, bit) + shape[axis + 1 :]
        b = a.reshape(split)
        a = jnp.where((me & bit) != 0, jnp.flip(b, axis + 1), b).reshape(shape)
        bit *= 2
    return a


def flip(a, k):
    bit = 1
    while bit <= k:
        if k & bit:
            a = a + bit - 2 * bit * ((a // bit) % 2)
        bit *= 2
    return a


def x_size(shards):
    x = 1
    while 2 * x * 2 * x <= shards:
        x *= 2
    return x


def score_block(logits, target, first, out_ref):
    count, vocab = logits.shape
    row_max = jnp.max(logits, axis=1, keepdims=True)
    exp_total = jnp.sum(jnp.exp(logits - row_max), axis=1, keepdims=True)
    column = lax.broadcasted_iota(jnp.int32, (count, vocab), 1) + first
    picked = jnp.sum(jnp.where(column == target, logits, 0.0), axis=1, keepdims=True)
    lane = lax.broadcasted_iota(jnp.int32, (count, 128), 1)
    packed = jnp.where(lane == 0, row_max, jnp.where(lane == 1, exp_total, picked))
    out_ref[0] = packed.T[:8]


def exchange_kernel(
    shards, ways, rows_ref, weight_ref, target_ref, held, near, far, part, stats,
    w_near, w_far,
    y_sems, z_sems, x_sems, c_sems, w_sems, f_sems, local_sems,
):
    me = lax.axis_index("dp")
    place = lax.axis_index("mp")
    x_ways = x_size(shards)
    z_ways = shards // x_ways
    halves = ways // 2
    slots, width = rows_ref.shape
    tokens = held.shape[1]
    vocab = near.shape[1]
    cuts, _, _, cut = far.shape

    peers = [{"mp": flip(place, k)} for k in range(1, ways)]
    peers += [{"dp": flip(me, z * x_ways)} for z in range(1, z_ways)]
    peers += [{"dp": flip(me, x)} for x in range(1, x_ways)]
    barrier = pltpu.get_barrier_semaphore()
    for peer in peers:
        pl.semaphore_signal(
            barrier, inc=1, device_id=peer, device_id_type=pl.DeviceIdType.MESH
        )
    pl.semaphore_wait(barrier, len(peers))

    started = []

    def send(src, dst, sems, i, peer):
        copy = pltpu.make_async_remote_copy(
            src_ref=src,
            dst_ref=dst,
            send_sem=sems.at[0, i],
            recv_sem=sems.at[1, i],
            device_id=peer,
            device_id_type=pl.DeviceIdType.MESH,
        )
        copy.start()
        started.append(copy)
        return copy

    def slot(k, r, count=1):
        return held.at[k, pl.ds(r * slots, count * slots), :]

    def columns(k, first=0, count=vocab):
        start = pl.multiple_of(flip(place, k) * vocab + first, count)
        return weight_ref.at[:, pl.ds(start, count)]

    def send_far(c):
        for k in range(2, ways):
            far_copy[c, k] = send(
                columns(k, c * cut, cut), far.at[c, k - 2], f_sems, c * ways + k,
                {"mp": flip(place, k)},
            )

    own_rows = pltpu.make_async_copy(rows_ref, slot(0, 0), local_sems.at[0])
    own_rows.start()
    y_copy, z_copy, x_copy, c_copy, far_copy = {}, {}, {}, {}, {}
    for m in range(1, halves):
        y_copy[m] = send(rows_ref, slot(2 * m, 0), y_sems, m, {"mp": flip(place, 2 * m)})
    for c in range(max(1, cuts - 1)):
        send_far(c)
    near_copy = send(columns(1), near, w_sems, 0, {"mp": flip(place, 1)})
    own_weight = pltpu.make_async_copy(columns(0), w_near.at[0], local_sems.at[1])
    own_weight.start()

    def spread(m, z):
        src = rows_ref if m == 0 and z == 0 else slot(2 * m, z * x_ways)
        if z == 0:
            for z_to in range(1, z_ways):
                z_copy[m, z_to] = send(
                    src, slot(2 * m, z_to * x_ways), z_sems, m * z_ways + z_to,
                    {"dp": flip(me, z_to * x_ways)},
                )
        for x in range(1, x_ways):
            x_copy[m, z, x] = send(
                src, slot(2 * m, z * x_ways + x), x_sems, (m * z_ways + z) * x_ways + x,
                {"dp": flip(me, x)},
            )

    spread(0, 0)
    for m in range(1, halves):
        y_copy[m].wait_recv()
        spread(m, 0)
    for z in range(1, z_ways):
        for m in range(halves):
            z_copy[m, z].wait_recv()
            spread(m, z)
    if cuts > 1:
        send_far(cuts - 1)
    own_rows.wait()
    for z in range(z_ways):
        for m in range(halves):
            for x in range(1, x_ways):
                x_copy[m, z, x].wait_recv()
            c_copy[m, z] = send(
                slot(2 * m, z * x_ways, x_ways), slot(2 * m + 1, z * x_ways, x_ways),
                c_sems, m * z_ways + z, {"mp": flip(place, 1)},
            )
    own_weight.wait()
    near_copy.wait_recv()
    near_weight = pltpu.make_async_copy(near, w_near.at[1], local_sems.at[2])
    near_weight.start()
    near_weight.wait()
    for c in c_copy.values():
        c.wait_recv()

    block = 256
    steps = (tokens // block,)
    row_spec = pl.BlockSpec((block, width), lambda i: (i, 0))

    def multiply(a_ref, b_ref, out_ref):
        out_ref[...] = jnp.dot(
            a_ref[...], w_near[0], preferred_element_type=jnp.float32
        ) + jnp.dot(b_ref[...], w_near[1], preferred_element_type=jnp.float32)

    pltpu.emit_pipeline(
        multiply,
        grid=steps,
        in_specs=[row_spec] * 2,
        out_specs=[pl.BlockSpec((block, vocab), lambda i: (i, 0))],
    )(held.at[0], held.at[1], part)

    for c in range(cuts):
        for k in range(2, ways):
            far_copy[c, k].wait_recv()
        load = pltpu.make_async_copy(far.at[c], w_far, local_sems.at[3])
        load.start()
        load.wait()

        def score(part_block, target_block, *refs, first=c * cut):
            logits = part_block[...]
            for k in range(ways - 2):
                logits += jnp.dot(refs[k][...], w_far[k], preferred_element_type=jnp.float32)
            score_block(logits, target_block[...], first, refs[-1])

        pltpu.emit_pipeline(
            score,
            grid=steps,
            in_specs=[
                pl.BlockSpec((block, cut), functools.partial(lambda c, i: (i, c), c)),
                pl.BlockSpec((block, 1), lambda i: (i, 0)),
            ]
            + [row_spec] * (ways - 2),
            out_specs=[pl.BlockSpec((1, 8, block), functools.partial(lambda c, i: (c, 0, i), c))],
        )(part, target_ref, *[held.at[k] for k in range(2, ways)], stats)
    for copy in started:
        copy.wait_send()


def score_rows(rows, head_weight, target, shards, ways):
    slots, width = rows.shape
    tokens = shards * slots
    vocab = head_weight.shape[1] // ways
    halves = ways // 2
    cut = min(vocab, 512)
    cuts = vocab // cut
    pairs = lambda count: pltpu.SemaphoreType.DMA((2, count))
    return pl.pallas_call(
        functools.partial(exchange_kernel, shards, ways),
        in_specs=[pl.BlockSpec(memory_space=pl.ANY)] * 3,
        out_specs=[pl.BlockSpec(memory_space=pl.ANY)] * 5,
        out_shape=[
            jax.ShapeDtypeStruct((ways, tokens, width), rows.dtype),
            jax.ShapeDtypeStruct((width, vocab), head_weight.dtype),
            jax.ShapeDtypeStruct((cuts, ways - 2, width, cut), head_weight.dtype),
            jax.ShapeDtypeStruct((tokens, vocab), jnp.float32),
            jax.ShapeDtypeStruct((cuts, 8, tokens), jnp.float32),
        ],
        scratch_shapes=[
            pltpu.VMEM((2, width, vocab), head_weight.dtype),
            pltpu.VMEM((ways - 2, width, cut), head_weight.dtype),
            pairs(halves),
            pairs(halves * shards),
            pairs(halves * shards),
            pairs(halves * shards),
            pairs(1),
            pairs(cuts * ways),
            pltpu.SemaphoreType.DMA((4,)),
        ],
        compiler_params=pltpu.CompilerParams(
            collective_id=0, has_side_effects=True, vmem_limit_bytes=48 * 1024 * 1024
        ),
        cost_estimate=pl.CostEstimate(
            flops=2 * ways * tokens * vocab * width,
            bytes_accessed=2 * ways * width * (tokens + vocab) + 8 * tokens * vocab,
            transcendentals=tokens * vocab,
        ),
    )(rows, head_weight, target)[4]


def combine_stats(stats):
    top = jnp.max(stats[:, 0], axis=0)
    total = jnp.sum(stats[:, 1] * jnp.exp(stats[:, 0] - top[None]), axis=0)
    return jnp.stack([top, total, jnp.sum(stats[:, 2], axis=0)])


def body(
    token_ids,
    lengths,
    pack_dest,
    ref_hidden,
    reward_hidden,
    head_weight,
    norm_gain,
    score_weight,
    value_weight,
    old_logprob,
):
    shards = lax.axis_size("dp")
    ways = lax.axis_size("mp")
    me = lax.axis_index("dp")
    part_index = lax.axis_index("mp")
    req_dev, max_len, width = ref_hidden.shape
    slots = req_dev // 2 * (max_len + 1)
    per_pair = req_dev // shards
    run = slots // shards
    tokens = shards * slots
    vocab_row = head_weight.shape[1]
    vocab = vocab_row // ways

    dest = xor_order(pack_dest.reshape(shards, req_dev), 0, me)
    lens = xor_order(lengths.reshape(shards, req_dev), 0, me)
    ids = xor_order(token_ids.reshape(shards, req_dev * max_len), 0, me)
    index = jnp.arange(req_dev, dtype=jnp.int32)
    order = dest * req_dev + index[None]
    before = order[:, None, :] < order[:, :, None]
    offsets = jnp.sum(jnp.where(before, lens[:, None, :], 0), axis=2)
    inner = jnp.arange(max_len, dtype=jnp.int32)
    valid = inner < lens[:, :, None]
    place = jnp.where(valid, offsets[:, :, None] + inner, -1).reshape(shards, -1)
    last = (inner == lens[:, :, None] - 1).reshape(shards, -1)
    slot_ids = jnp.arange(slots, dtype=jnp.int32)
    chosen = place[:, None, :] == slot_ids[None, :, None]
    target_last = jnp.sum(
        jnp.where(chosen, (2 * ids + last.astype(jnp.int32))[:, None, :], 0), axis=2
    )
    targets = target_last >> 1
    is_last = target_last & 1

    own_chosen = chosen[0]
    rows = jnp.dot(
        own_chosen.astype(jnp.bfloat16),
        ref_hidden.reshape(req_dev * max_len, width),
        preferred_element_type=jnp.float32,
    ).astype(jnp.bfloat16)
    hidden = reward_hidden.reshape(req_dev * max_len, width).astype(jnp.float32)
    sums = jnp.stack(
        [
            jnp.sum(hidden * hidden, axis=1),
            jnp.sum(hidden * (norm_gain * score_weight), axis=1),
            jnp.sum(hidden * (norm_gain * value_weight), axis=1),
        ]
    )
    sums = jnp.sum(jnp.where(own_chosen[None], sums[:, None, :], 0.0), axis=2)
    my_last = lax.dynamic_slice(
        xor_order(is_last, 0, me), (0, me * run), (shards, run)
    ).reshape(slots)
    not_last = 1.0 - my_last.astype(jnp.float32)
    base = me * vocab_row + part_index * vocab
    stats = score_rows(
        rows, head_weight, (targets - base).reshape(tokens, 1), shards, ways
    )
    stats = combine_stats(stats[:, :3])

    stats = xor_order(stats.reshape(3, shards, shards, run), 1, me)
    sent = jnp.concatenate([stats, sums.reshape(3, 1, shards, run)], axis=1)
    taken = lax.all_to_all(jnp.transpose(sent, (2, 0, 1, 3)), "dp", 0, 0, tiled=True)
    stats = combine_stats(taken[:, :, :shards].reshape(shards, 3, slots))
    sums = jnp.transpose(taken[:, :, shards], (1, 0, 2)).reshape(3, slots)
    gathered = lax.all_gather(jnp.concatenate([stats, sums]), "mp")
    stats = combine_stats(gathered[:, :3])
    sums = jnp.sum(gathered[:, 3:], axis=0)
    ref_logprob = stats[2] - stats[0] - jnp.log(stats[1])

    inv_rms = lax.rsqrt(sums[0] / (width * ways) + norm_eps)
    score = sums[1] * inv_rms
    value_est = sums[2] * inv_rms
    next_value = jnp.concatenate([value_est[1:], jnp.zeros((1,), jnp.float32)])
    reward = -kl_coef * (old_logprob - ref_logprob) + jnp.where(my_last != 0, score, 0.0)
    td_error = reward + discount * next_value * not_last - value_est
    decay = discount * gae_mix * not_last
    advantage = td_error
    for _ in range(max_len - 1):
        following = jnp.concatenate([advantage[1:], jnp.zeros((1,), jnp.float32)])
        advantage = td_error + decay * following
    return (ref_logprob, advantage)


def solution(mesh):
    return jax.shard_map(
        body,
        mesh=mesh,
        in_specs=(
            P(),
            P(),
            P(),
            P("dp", None, "mp"),
            P("dp", None, "mp"),
            P("mp", "dp"),
            P("mp"),
            P("mp"),
            P("mp"),
            P("dp"),
        ),
        out_specs=(P("dp"), P("dp")),
        check_vma=False,
    )
```

```python
import functools

import jax
import jax.numpy as jnp
from jax import lax
from jax.experimental import pallas as pl
from jax.experimental.pallas import tpu as pltpu
from jax.sharding import PartitionSpec as P

kl_coef = 0.1
discount = 0.99
gae_mix = 0.95
norm_eps = 1e-05


def xor_order(a, axis, me):
    size = a.shape[axis]
    bit = 1
    while bit < size:
        shape = a.shape
        split = shape[:axis] + (size // (2 * bit), 2, bit) + shape[axis + 1 :]
        b = a.reshape(split)
        a = jnp.where((me & bit) != 0, jnp.flip(b, axis + 1), b).reshape(shape)
        bit *= 2
    return a


def flip(a, k):
    bit = 1
    while bit <= k:
        if k & bit:
            a = a + bit - 2 * bit * ((a // bit) % 2)
        bit *= 2
    return a


def x_size(shards):
    x = 1
    while 2 * x * 2 * x <= shards:
        x *= 2
    return x


def score_block(logits, target, first, out_ref):
    count, vocab = logits.shape
    row_max = jnp.max(logits, axis=1, keepdims=True)
    exp_total = jnp.sum(jnp.exp(logits - row_max), axis=1, keepdims=True)
    column = lax.broadcasted_iota(jnp.int32, (count, vocab), 1) + first
    picked = jnp.sum(jnp.where(column == target, logits, 0.0), axis=1, keepdims=True)
    lane = lax.broadcasted_iota(jnp.int32, (count, 128), 1)
    packed = jnp.where(lane == 0, row_max, jnp.where(lane == 1, exp_total, picked))
    out_ref[0] = packed.T[:8]


def exchange_kernel(
    shards, ways, rows_ref, weight_ref, target_ref, held, near, far, part, stats,
    w_near, w_far,
    y_sems, z_sems, x_sems, c_sems, w_sems, f_sems, local_sems,
):
    me = lax.axis_index("dp")
    place = lax.axis_index("mp")
    x_ways = x_size(shards)
    z_ways = shards // x_ways
    halves = ways // 2
    slots, width = rows_ref.shape
    tokens = held.shape[1]
    vocab = near.shape[1]
    cuts, _, _, cut = far.shape

    peers = [{"mp": flip(place, k)} for k in range(1, ways)]
    peers += [{"dp": flip(me, z * x_ways)} for z in range(1, z_ways)]
    peers += [{"dp": flip(me, x)} for x in range(1, x_ways)]
    barrier = pltpu.get_barrier_semaphore()
    for peer in peers:
        pl.semaphore_signal(
            barrier, inc=1, device_id=peer, device_id_type=pl.DeviceIdType.MESH
        )
    pl.semaphore_wait(barrier, len(peers))

    started = []

    def send(src, dst, sems, i, peer):
        copy = pltpu.make_async_remote_copy(
            src_ref=src,
            dst_ref=dst,
            send_sem=sems.at[0, i],
            recv_sem=sems.at[1, i],
            device_id=peer,
            device_id_type=pl.DeviceIdType.MESH,
        )
        copy.start()
        started.append(copy)
        return copy

    def slot(k, r, count=1):
        return held.at[k, pl.ds(r * slots, count * slots), :]

    def columns(k, first=0, count=vocab):
        start = pl.multiple_of(flip(place, k) * vocab + first, count)
        return weight_ref.at[:, pl.ds(start, count)]

    def send_far(c):
        for k in range(2, ways):
            far_copy[c, k] = send(
                columns(k, c * cut, cut), far.at[c, k - 2], f_sems, c * ways + k,
                {"mp": flip(place, k)},
            )

    own_rows = pltpu.make_async_copy(rows_ref, slot(0, 0), local_sems.at[0])
    own_rows.start()
    y_copy, z_copy, x_copy, c_copy, far_copy = {}, {}, {}, {}, {}
    for m in range(1, halves):
        y_copy[m] = send(rows_ref, slot(2 * m, 0), y_sems, m, {"mp": flip(place, 2 * m)})
    for c in range(max(1, cuts - 1)):
        send_far(c)
    near_copy = send(columns(1), near, w_sems, 0, {"mp": flip(place, 1)})
    own_weight = pltpu.make_async_copy(columns(0), w_near.at[0], local_sems.at[1])
    own_weight.start()

    def spread(m, z):
        src = rows_ref if m == 0 and z == 0 else slot(2 * m, z * x_ways)
        if z == 0:
            for z_to in range(1, z_ways):
                z_copy[m, z_to] = send(
                    src, slot(2 * m, z_to * x_ways), z_sems, m * z_ways + z_to,
                    {"dp": flip(me, z_to * x_ways)},
                )
        for x in range(1, x_ways):
            x_copy[m, z, x] = send(
                src, slot(2 * m, z * x_ways + x), x_sems, (m * z_ways + z) * x_ways + x,
                {"dp": flip(me, x)},
            )

    spread(0, 0)
    for m in range(1, halves):
        y_copy[m].wait_recv()
        spread(m, 0)
    for z in range(1, z_ways):
        for m in range(halves):
            z_copy[m, z].wait_recv()
            spread(m, z)
    own_rows.wait()
    for z in range(z_ways):
        for m in range(halves):
            for x in range(1, x_ways):
                x_copy[m, z, x].wait_recv()
            c_copy[m, z] = send(
                slot(2 * m, z * x_ways, x_ways), slot(2 * m + 1, z * x_ways, x_ways),
                c_sems, m * z_ways + z, {"mp": flip(place, 1)},
            )
    if cuts > 1:
        send_far(cuts - 1)
    own_weight.wait()
    near_copy.wait_recv()
    near_weight = pltpu.make_async_copy(near, w_near.at[1], local_sems.at[2])
    near_weight.start()
    near_weight.wait()
    for c in c_copy.values():
        c.wait_recv()

    block = 256
    steps = (tokens // block,)
    row_spec = pl.BlockSpec((block, width), lambda i: (i, 0))

    def multiply(a_ref, b_ref, out_ref):
        out_ref[...] = jnp.dot(
            a_ref[...], w_near[0], preferred_element_type=jnp.float32
        ) + jnp.dot(b_ref[...], w_near[1], preferred_element_type=jnp.float32)

    pltpu.emit_pipeline(
        multiply,
        grid=steps,
        in_specs=[row_spec] * 2,
        out_specs=[pl.BlockSpec((block, vocab), lambda i: (i, 0))],
    )(held.at[0], held.at[1], part)

    for c in range(cuts):
        for k in range(2, ways):
            far_copy[c, k].wait_recv()
        load = pltpu.make_async_copy(far.at[c], w_far, local_sems.at[3])
        load.start()
        load.wait()

        def score(part_block, target_block, *refs, first=c * cut):
            logits = part_block[...]
            for k in range(ways - 2):
                logits += jnp.dot(refs[k][...], w_far[k], preferred_element_type=jnp.float32)
            score_block(logits, target_block[...], first, refs[-1])

        pltpu.emit_pipeline(
            score,
            grid=steps,
            in_specs=[
                pl.BlockSpec((block, cut), functools.partial(lambda c, i: (i, c), c)),
                pl.BlockSpec((block, 1), lambda i: (i, 0)),
            ]
            + [row_spec] * (ways - 2),
            out_specs=[pl.BlockSpec((1, 8, block), functools.partial(lambda c, i: (c, 0, i), c))],
        )(part, target_ref, *[held.at[k] for k in range(2, ways)], stats)
    for copy in started:
        copy.wait_send()


def score_rows(rows, head_weight, target, shards, ways):
    slots, width = rows.shape
    tokens = shards * slots
    vocab = head_weight.shape[1] // ways
    halves = ways // 2
    cut = min(vocab, 256)
    cuts = vocab // cut
    pairs = lambda count: pltpu.SemaphoreType.DMA((2, count))
    return pl.pallas_call(
        functools.partial(exchange_kernel, shards, ways),
        in_specs=[pl.BlockSpec(memory_space=pl.ANY)] * 3,
        out_specs=[pl.BlockSpec(memory_space=pl.ANY)] * 5,
        out_shape=[
            jax.ShapeDtypeStruct((ways, tokens, width), rows.dtype),
            jax.ShapeDtypeStruct((width, vocab), head_weight.dtype),
            jax.ShapeDtypeStruct((cuts, ways - 2, width, cut), head_weight.dtype),
            jax.ShapeDtypeStruct((tokens, vocab), jnp.float32),
            jax.ShapeDtypeStruct((cuts, 8, tokens), jnp.float32),
        ],
        scratch_shapes=[
            pltpu.VMEM((2, width, vocab), head_weight.dtype),
            pltpu.VMEM((ways - 2, width, cut), head_weight.dtype),
            pairs(halves),
            pairs(halves * shards),
            pairs(halves * shards),
            pairs(halves * shards),
            pairs(1),
            pairs(cuts * ways),
            pltpu.SemaphoreType.DMA((4,)),
        ],
        compiler_params=pltpu.CompilerParams(
            collective_id=0, has_side_effects=True, vmem_limit_bytes=48 * 1024 * 1024
        ),
        cost_estimate=pl.CostEstimate(
            flops=2 * ways * tokens * vocab * width,
            bytes_accessed=2 * ways * width * (tokens + vocab) + 8 * tokens * vocab,
            transcendentals=tokens * vocab,
        ),
    )(rows, head_weight, target)[4]


def combine_stats(stats):
    top = jnp.max(stats[:, 0], axis=0)
    total = jnp.sum(stats[:, 1] * jnp.exp(stats[:, 0] - top[None]), axis=0)
    return jnp.stack([top, total, jnp.sum(stats[:, 2], axis=0)])


def body(
    token_ids,
    lengths,
    pack_dest,
    ref_hidden,
    reward_hidden,
    head_weight,
    norm_gain,
    score_weight,
    value_weight,
    old_logprob,
):
    shards = lax.axis_size("dp")
    ways = lax.axis_size("mp")
    me = lax.axis_index("dp")
    part_index = lax.axis_index("mp")
    req_dev, max_len, width = ref_hidden.shape
    slots = req_dev // 2 * (max_len + 1)
    per_pair = req_dev // shards
    run = slots // shards
    tokens = shards * slots
    vocab_row = head_weight.shape[1]
    vocab = vocab_row // ways

    dest = xor_order(pack_dest.reshape(shards, req_dev), 0, me)
    lens = xor_order(lengths.reshape(shards, req_dev), 0, me)
    ids = xor_order(token_ids.reshape(shards, req_dev * max_len), 0, me)
    index = jnp.arange(req_dev, dtype=jnp.int32)
    order = dest * req_dev + index[None]
    before = order[:, None, :] < order[:, :, None]
    offsets = jnp.sum(jnp.where(before, lens[:, None, :], 0), axis=2)
    inner = jnp.arange(max_len, dtype=jnp.int32)
    valid = inner < lens[:, :, None]
    place = jnp.where(valid, offsets[:, :, None] + inner, -1).reshape(shards, -1)
    last = (inner == lens[:, :, None] - 1).reshape(shards, -1)
    slot_ids = jnp.arange(slots, dtype=jnp.int32)
    chosen = place[:, None, :] == slot_ids[None, :, None]
    target_last = jnp.sum(
        jnp.where(chosen, (2 * ids + last.astype(jnp.int32))[:, None, :], 0), axis=2
    )
    targets = target_last >> 1
    is_last = target_last & 1

    own_chosen = chosen[0]
    rows = jnp.dot(
        own_chosen.astype(jnp.bfloat16),
        ref_hidden.reshape(req_dev * max_len, width),
        preferred_element_type=jnp.float32,
    ).astype(jnp.bfloat16)
    hidden = reward_hidden.reshape(req_dev * max_len, width).astype(jnp.float32)
    sums = jnp.stack(
        [
            jnp.sum(hidden * hidden, axis=1),
            jnp.sum(hidden * (norm_gain * score_weight), axis=1),
            jnp.sum(hidden * (norm_gain * value_weight), axis=1),
        ]
    )
    sums = jnp.sum(jnp.where(own_chosen[None], sums[:, None, :], 0.0), axis=2)
    my_last = lax.dynamic_slice(
        xor_order(is_last, 0, me), (0, me * run), (shards, run)
    ).reshape(slots)
    not_last = 1.0 - my_last.astype(jnp.float32)
    base = me * vocab_row + part_index * vocab
    stats = score_rows(
        rows, head_weight, (targets - base).reshape(tokens, 1), shards, ways
    )
    stats = combine_stats(stats[:, :3])

    stats = xor_order(stats.reshape(3, shards, shards, run), 1, me)
    sent = jnp.concatenate([stats, sums.reshape(3, 1, shards, run)], axis=1)
    taken = lax.all_to_all(jnp.transpose(sent, (2, 0, 1, 3)), "dp", 0, 0, tiled=True)
    stats = combine_stats(taken[:, :, :shards].reshape(shards, 3, slots))
    sums = jnp.transpose(taken[:, :, shards], (1, 0, 2)).reshape(3, slots)
    gathered = lax.all_gather(jnp.concatenate([stats, sums]), "mp")
    stats = combine_stats(gathered[:, :3])
    sums = jnp.sum(gathered[:, 3:], axis=0)
    ref_logprob = stats[2] - stats[0] - jnp.log(stats[1])

    inv_rms = lax.rsqrt(sums[0] / (width * ways) + norm_eps)
    score = sums[1] * inv_rms
    value_est = sums[2] * inv_rms
    next_value = jnp.concatenate([value_est[1:], jnp.zeros((1,), jnp.float32)])
    reward = -kl_coef * (old_logprob - ref_logprob) + jnp.where(my_last != 0, score, 0.0)
    td_error = reward + discount * next_value * not_last - value_est
    decay = discount * gae_mix * not_last
    advantage = td_error
    for _ in range(max_len - 1):
        following = jnp.concatenate([advantage[1:], jnp.zeros((1,), jnp.float32)])
        advantage = td_error + decay * following
    return (ref_logprob, advantage)


def solution(mesh):
    return jax.shard_map(
        body,
        mesh=mesh,
        in_specs=(
            P(),
            P(),
            P(),
            P("dp", None, "mp"),
            P("dp", None, "mp"),
            P("mp", "dp"),
            P("mp"),
            P("mp"),
            P("mp"),
            P("dp"),
        ),
        out_specs=(P("dp"), P("dp")),
        check_vma=False,
    )
```
